32 devices in a mesh: members: 2 (over y), shard: 4 (over z), dp: 4 (over x, core).
Axes of the slice: x: 2, y: 2, z: 4, core: 2. Of those that a mesh axis runs over, the one named last changes fastest.
Arguments:
- table: bfloat16 [1024, 3072], P(None, 'shard'), may hold values from -6 to 6
- indices: int32 [8192], P(('members', 'dp')), parts along dimension 0, may hold values from 0 to 1023
- grad_out: bfloat16 [8192, 8192], P(('members', 'dp'), 'shard'), parts along dimension 0, may hold values from -6 to 6
- mean: float32 [6144, 8192], P(('members', 'dp'), 'shard'), parts along dimension 0, may hold values from -6 to 6
- precision: float32 [6144, 8192], P(('members', 'dp'), 'shard'), parts along dimension 0, may hold values from 0.3 to 3
- block_salts: int32 [32], P('members'), parts along dimension 0, may hold values from 0 to 1073741823
Outputs:
- new_mean: float32 [6144, 8192], P(('members', 'dp'), 'shard'), parts along dimension 0
- new_precision: float32 [6144, 8192], P(('members', 'dp'), 'shard'), parts along dimension 0
The draws below stay inside these ranges and needn't reach their ends.
There are 2 independent parts, one for each index of `members`. The reference program is written for one: setup_inputs(seed, part) draws one part's arguments, and reference() takes and returns one part's arrays. A program takes and returns all parts, laid end to end along the dimension named above; an argument that names none is the same for every part. Nothing has to cross between parts.
All inputs are finite; a program needn't handle non-finite values.
Results may differ from the reference program's by a relative error of at most 0.0035.
Values may be sent and summed in bfloat16 or wider, within the bound.
No kernel may reach another device: no remote copies, remote signals or barrier semaphores. Data moves between devices by JAX's collectives and lax.ppermute only.
A program may use at most 192 MiB of HBM per device.

```python
import math
import jax
import jax.numpy as jnp
import numpy as np
from jax import lax

D = 3072
FF = 8192
TABLE = 1024
B_DEV = 1024
B_TOTAL = 4096
SALT_COUNT = 16
N_SHARD = 4
N_DP = 4


def plant(values, stream_key, low, largest):
    longest = values.shape.index(max(values.shape))
    spots = []
    for shift in (0, 1):
        where = [jax.random.randint(jax.random.fold_in(stream_key, axis), (), 0, length) for axis, length in enumerate(values.shape)]
        where[longest] = (where[longest] + shift) % values.shape[longest]
        spots.append(tuple(where))
    return values.at[spots[0]].set(low).at[spots[1]].set(largest)


def levels(own_key, dims, shards, least, largest):
    loudness, own = 1.0, jax.random.fold_in(own_key, 6)
    for dim, parts in shards:
        steps = jnp.exp(jax.random.uniform(jax.random.fold_in(own, dim), (parts,), jnp.float32, least / len(shards), largest / len(shards)))
        loudness = loudness * jnp.repeat(steps, dims[dim] // parts).reshape([-1 if axis == dim else 1 for axis in range(len(dims))])
    return loudness


def rank_table(count, lean):
    weights = [(1 << 20) // math.isqrt(rank ** lean) + 1 for rank in range(1, count + 1)]
    scale = 1 + sum(weights) // (1 << 30)
    return np.cumsum(np.array([max(1, weight // scale) for weight in weights]))


def ranked_ids(own_key, dims, count, skew):
    listing = rank_table(count, skew)
    lot = jax.random.randint(jax.random.fold_in(own_key, 1), dims, 0, int(listing[count - 1]))
    rank = jnp.searchsorted(jnp.asarray(listing, jnp.int32), lot, side="right")
    return jax.random.permutation(jax.random.fold_in(own_key, 2), count)[rank].astype(jnp.int32)


def centred(key, extent, width, reach, split=(), held_as=jnp.bfloat16):
    gain = levels(key, extent, split, -0.22, 0.18) if split else 1.0
    entries = jax.random.normal(key, extent, jnp.float32) * width * gain
    return jnp.minimum(jnp.maximum(entries, -reach), reach).astype(held_as)


def setup_inputs(seed: int = 0, part: int = 0) -> dict:
    keys = jax.random.split(jax.random.key(seed), 7)
    part_splits = jax.random.split(jax.random.fold_in(keys[6], part), 7)
    return {
        "table": centred(keys[0], (TABLE, D), 1.0, 6.0, ((1, 4),)),
        "indices": plant(ranked_ids(part_splits[1], (B_TOTAL,), TABLE, 2), jax.random.fold_in(part_splits[1], 3), 0, TABLE - 1).astype(jnp.int32),
        "grad_out": centred(part_splits[2], (B_TOTAL, FF), 1.0, 6.0, ((0, 4), (1, 4))),
        "mean": centred(part_splits[3], (D, FF), 1.0, 6.0, ((0, 4), (1, 4)), jnp.float32),
        "precision": jnp.clip(jnp.exp(math.log(3.0) - 2.3025851 * jax.random.uniform(part_splits[4], (D, FF), jnp.float32) ** levels(part_splits[4], (D, FF), ((0, 4), (1, 4)), -0.2, 0.2)), 0.3, 3.0),
        "block_salts": plant(jax.random.randint(part_splits[5], (SALT_COUNT,), 0, 1073741824), jax.random.fold_in(part_splits[5], 1), 0, 1073741823).astype(jnp.int32),
    }


def hashed_noise(rows, cols, salt_value, full_ff):
    value = rows * full_ff + cols
    mixed = jnp.bitwise_xor(value, salt_value)
    mixed = mixed * 73244475
    mixed = jnp.bitwise_xor(mixed, jnp.right_shift(jnp.bitwise_and(mixed, 2147483647), 16))
    mixed = mixed * 73244475
    mixed = jnp.bitwise_xor(mixed, jnp.right_shift(jnp.bitwise_and(mixed, 2147483647), 16))
    kept = jnp.right_shift(jnp.bitwise_and(mixed, 2147483647), 7).astype(jnp.float32)
    return 1.7320508075688772 * (2.0 * (kept + 0.5) / 16777216.0 - 1.0)

def reference(table, indices, grad_out, mean, precision, block_salts):
    rows_blk = D // N_DP
    cols_blk = FF // N_SHARD
    rows = jnp.arange(D, dtype=jnp.int32)[:, None]
    cols = jnp.arange(FF, dtype=jnp.int32)[None, :]
    block = rows // rows_blk * N_SHARD + cols // cols_blk
    salt_grid = jnp.take(block_salts, block.astype(jnp.int32))
    noise = hashed_noise(rows, cols, salt_grid, FF)
    theta = mean + 0.5 * noise / jnp.sqrt(precision + 0.1)
    weight = (theta / jnp.sqrt(jnp.float32(D))).astype(jnp.bfloat16)
    weight_wide = weight.astype(jnp.float32)
    feats = jnp.take(table, indices, axis=0)
    feats_groups = feats.reshape(N_DP, B_DEV, D)
    out_groups = grad_out.reshape(N_DP, B_DEV, FF)
    inv_root = 1.0 / jnp.sqrt(jnp.float32(D))
    inv_width = 1.0 / jnp.float32(D)

    def step(carry, group):
        feats_g, out_g = group
        feats_w = feats_g.astype(jnp.float32)
        pre = jnp.dot(feats_w, weight_wide)
        sig = jax.nn.sigmoid(pre)
        slope = (out_g.astype(jnp.float32) * sig * (1.0 + pre * (1.0 - sig))).astype(jnp.bfloat16)
        slope_w = slope.astype(jnp.float32)
        slope_sq = (slope_w * slope_w).astype(jnp.bfloat16).astype(jnp.float32)
        feats_sq = (feats_w * feats_w).astype(jnp.bfloat16).astype(jnp.float32)
        part_grad = (jnp.dot(feats_w.T, slope_w) * inv_root).astype(jnp.bfloat16)
        part_sq = (jnp.dot(feats_sq.T, slope_sq) * inv_width).astype(jnp.bfloat16)
        return ((carry[0] + part_grad.astype(jnp.float32), carry[1] + part_sq.astype(jnp.float32)), None)
    zeros = jnp.zeros((D, FF), jnp.float32)
    (grad, sq_sum), unused = lax.scan(step, (zeros, zeros), (feats_groups, out_groups))
    new_precision = 0.7 * precision + 0.3 * sq_sum
    new_mean = mean - 0.5 * (grad + 0.1 * mean) / (new_precision + 0.1)
    return (new_mean, new_precision)
```

```python
import functools

import jax
import jax.numpy as jnp
from jax import lax
from jax.sharding import PartitionSpec as P

F32 = jnp.float32
BF16 = jnp.bfloat16


def hashed_noise(rows, cols, salt_value, full_ff):
    value = rows * full_ff + cols
    mixed = jnp.bitwise_xor(value, salt_value)
    mixed = mixed * 73244475
    mixed = jnp.bitwise_xor(mixed, jnp.right_shift(jnp.bitwise_and(mixed, 2147483647), 16))
    mixed = mixed * 73244475
    mixed = jnp.bitwise_xor(mixed, jnp.right_shift(jnp.bitwise_and(mixed, 2147483647), 16))
    kept = jnp.right_shift(jnp.bitwise_and(mixed, 2147483647), 7).astype(jnp.float32)
    return 1.7320508075688772 * (2.0 * (kept + 0.5) / 16777216.0 - 1.0)


def sample_block(mean_rows, prec_rows, row_start, col_start, salt_rows, full_ff, inv_root):
    rows = row_start + jnp.arange(mean_rows.shape[0], dtype=jnp.int32)[:, None]
    cols = col_start + jnp.arange(mean_rows.shape[1], dtype=jnp.int32)[None, :]
    noise = hashed_noise(rows, cols, salt_rows, full_ff)
    theta = mean_rows + 0.5 * noise / jnp.sqrt(prec_rows + 0.1)
    return (theta * inv_root).astype(BF16)


def dot(a, b):
    return jnp.dot(a, b, preferred_element_type=F32)


def dot_t(a, b):
    return lax.dot_general(a, b, (((0,), (0,)), ((), ())), preferred_element_type=F32)


def square(a):
    wide = a.astype(F32)
    return (wide * wide).astype(BF16)


def one_hot(idx, n_rows):
    return (idx[:, None] == jnp.arange(n_rows, dtype=jnp.int32)[None, :]).astype(BF16)


def row_sums(idx, go, n_rows):
    hot = one_hot(idx, n_rows)
    return dot_t(hot, go), dot_t(hot, square(go))


def slopes(pre, total, total_sq):
    sig = jax.nn.sigmoid(pre)
    h = sig * (1.0 + pre * (1.0 - sig))
    return (h * total).astype(BF16), (h * h * total_sq).astype(BF16)


def update(grad, sq_sum, mean, precision):
    new_precision = 0.7 * precision + 0.3 * sq_sum
    new_mean = mean - 0.5 * (grad + 0.1 * mean) / (new_precision + 0.1)
    return new_mean, new_precision


def own_sample(mean, precision, block_salts, dp_pos, shard_pos, n_shard, width):
    rows_blk, cols_blk = mean.shape
    inv_root = 1.0 / jnp.sqrt(F32(width))
    salt = lax.dynamic_index_in_dim(block_salts, dp_pos * n_shard + shard_pos, 0, keepdims=False)
    return sample_block(
        mean, precision, dp_pos * rows_blk, shard_pos * cols_blk, salt, cols_blk * n_shard, inv_root
    )


def general(table, indices, grad_out, mean, precision, block_salts):
    n_dp, n_shard = lax.axis_size("dp"), lax.axis_size("shard")
    dp_pos, shard_pos = lax.axis_index("dp"), lax.axis_index("shard")
    n_rows, width = table.shape[0], table.shape[1] * n_shard
    rows_blk = mean.shape[0]
    whole = lax.all_gather(table, "shard", axis=1, tiled=True)
    tab = lax.dynamic_slice_in_dim(whole, dp_pos * rows_blk, rows_blk, 1)
    weight = own_sample(mean, precision, block_salts, dp_pos, shard_pos, n_shard, width)
    pre = lax.psum_scatter(dot(tab, weight), "dp", scatter_dimension=1, tiled=True)
    go = lax.all_to_all(grad_out, "dp", 1, 0, tiled=True)
    idx = lax.all_gather(indices, "dp", axis=0, tiled=True)
    s, s2 = slopes(pre, *row_sums(idx, go, n_rows))
    s = lax.all_gather(s, "dp", axis=1, tiled=True)
    s2 = lax.all_gather(s2, "dp", axis=1, tiled=True)
    grad = dot_t(tab, s) * (1.0 / jnp.sqrt(F32(width)))
    sq_sum = dot_t(square(tab), s2) * (1.0 / F32(width))
    return update(grad, sq_sum, mean, precision)


CORE = [(j, j ^ 1) for j in range(4)]
CHIP = [(j, j ^ 2) for j in range(4)]


def table_steps():
    low = [
        [((0, 0), (1, 0)), ((1, 0), (2, 1)), ((1, 1), (0, 1))],
        [((1, 0), (2, 0)), ((2, 1), (3, 1))],
        [((2, 0), (3, 0))],
    ]
    steps = []
    for moves in low:
        pairs = []
        for (z, c), (z2, c2) in moves:
            pairs.append((z * 4 + c, z2 * 4 + c2))
            pairs.append(((3 - z) * 4 + 3 - c, (3 - z2) * 4 + 3 - c2))
        steps.append(pairs)
    return steps


def fetch_table(table, dp_pos, shard_pos, pieces):
    rows = table.shape[0] // pieces
    steps = table_steps()
    out = []
    for k in range(pieces):
        own = table[k * rows : (k + 1) * rows]
        first = lax.ppermute(own, ("shard", "dp"), steps[0])
        second = lax.ppermute(first, ("shard", "dp"), steps[1])
        third = lax.ppermute(second, ("shard", "dp"), steps[2])
        got = jnp.where(shard_pos == dp_pos, own, first + second + third)
        out.append(got)
    return out


def on_device(table, indices, grad_out, mean, precision, block_salts):
    n_shard = lax.axis_size("shard")
    dp_pos, shard_pos = lax.axis_index("dp"), lax.axis_index("shard")
    n_rows, width = table.shape[0], table.shape[1] * n_shard
    part = mean.shape[1] // 4
    chunks = 2
    cut = part // chunks
    mine, other = dp_pos, dp_pos ^ 2

    def cols(a, owner, k=None):
        if k is None:
            return lax.dynamic_slice_in_dim(a, owner * part, part, 1)
        return lax.dynamic_slice_in_dim(a, owner * part + k * cut, cut, 1)

    idx_core = lax.ppermute(indices, "dp", CORE)
    idx_far = lax.ppermute(jnp.concatenate([indices, idx_core]), "dp", CHIP)
    go_far0 = lax.ppermute(cols(grad_out, other), "dp", CHIP)
    go_pass = lax.ppermute(cols(grad_out, other ^ 1), "dp", CORE)
    go_core = lax.ppermute(cols(grad_out, mine ^ 1), "dp", CORE)
    go_far1 = lax.ppermute(go_pass, "dp", CHIP)
    go_near = jnp.concatenate([cols(grad_out, mine), go_core], 0)
    idx_near = jnp.concatenate([indices, idx_core], 0)

    tabs = fetch_table(table, dp_pos, shard_pos, 2)
    tab = jnp.concatenate(tabs, 0)
    tab_core = jnp.concatenate([lax.ppermute(t, "dp", CORE) for t in tabs], 0)

    weight = own_sample(mean, precision, block_salts, dp_pos, shard_pos, n_shard, width)
    w_core_far = lax.ppermute(cols(weight, other ^ 1), "dp", CORE)
    w_core_near = lax.ppermute(cols(weight, mine ^ 1), "dp", CORE)
    w_far = cols(weight, other)
    w_near = cols(weight, mine)

    near_sums = row_sums(idx_near, go_near, n_rows)
    far_sums = row_sums(idx_far, jnp.concatenate([go_far0, go_far1], 0), n_rows)
    total = near_sums[0] + far_sums[0]
    total_sq = near_sums[1] + far_sums[1]
    pre_near = dot(tab, w_near) + dot(tab_core, w_core_near)

    pieces = []
    for k in range(chunks):
        c = slice(k * cut, (k + 1) * cut)
        out = (dot(tab, w_far[:, c]) + dot(tab_core, w_core_far[:, c])).astype(BF16)
        pre = pre_near[:, c] + lax.ppermute(out, "dp", CHIP).astype(F32)
        s, s2 = slopes(pre, total[:, c], total_sq[:, c])
        s_both = jnp.concatenate([s, s2], 0)
        far = lax.ppermute(s_both, "dp", CHIP)
        core = lax.ppermute(s_both, "dp", CORE)
        core_far = lax.ppermute(far, "dp", CORE)
        pieces.append((s_both, core, far, core_far))

    tab_sq = square(tab)
    inv_root = 1.0 / jnp.sqrt(F32(width))
    inv_width = 1.0 / F32(width)
    new_mean, new_precision = jnp.zeros_like(mean), jnp.zeros_like(precision)
    for n, flip in enumerate((0, 1, 2, 3)):
        for k in range(chunks):
            s_both = pieces[k][n]
            grad = dot_t(tab, s_both[:n_rows]) * inv_root
            sq_sum = dot_t(tab_sq, s_both[n_rows:]) * inv_width
            a, b = update(grad, sq_sum, cols(mean, mine ^ flip, k), cols(precision, mine ^ flip, k))
            start = (mine ^ flip) * part + k * cut
            new_mean = lax.dynamic_update_slice_in_dim(new_mean, a, start, 1)
            new_precision = lax.dynamic_update_slice_in_dim(new_precision, b, start, 1)
    return new_mean, new_precision


def solution(mesh):
    in_specs = (
        P(None, "shard"),
        P(("members", "dp")),
        P(("members", "dp"), "shard"),
        P(("members", "dp"), "shard"),
        P(("members", "dp"), "shard"),
        P("members"),
    )
    out_specs = (P(("members", "dp"), "shard"), P(("members", "dp"), "shard"))
    fits = mesh.shape["dp"] == 4 and mesh.shape["shard"] == 4
    return jax.shard_map(
        on_device if fits else general,
        mesh=mesh,
        in_specs=in_specs,
        out_specs=out_specs,
        check_vma=False,
    )
```

```python
import functools

import jax
import jax.numpy as jnp
from jax import lax
from jax.experimental import pallas as pl
from jax.experimental.pallas import tpu as pltpu
from jax.sharding import PartitionSpec as P

F32 = jnp.float32
BF16 = jnp.bfloat16


def hashed_noise(rows, cols, salt_value, full_ff):
    value = rows * full_ff + cols
    mixed = jnp.bitwise_xor(value, salt_value)
    mixed = mixed * 73244475
    mixed = jnp.bitwise_xor(mixed, jnp.right_shift(jnp.bitwise_and(mixed, 2147483647), 16))
    mixed = mixed * 73244475
    mixed = jnp.bitwise_xor(mixed, jnp.right_shift(jnp.bitwise_and(mixed, 2147483647), 16))
    kept = jnp.right_shift(jnp.bitwise_and(mixed, 2147483647), 7).astype(jnp.float32)
    return 1.7320508075688772 * (2.0 * (kept + 0.5) / 16777216.0 - 1.0)


def sample_block(mean_rows, prec_rows, row_start, col_start, salt_rows, full_ff, inv_root):
    rows = row_start + jnp.arange(mean_rows.shape[0], dtype=jnp.int32)[:, None]
    cols = col_start + jnp.arange(mean_rows.shape[1], dtype=jnp.int32)[None, :]
    noise = hashed_noise(rows, cols, salt_rows, full_ff)
    theta = mean_rows + 0.5 * noise / jnp.sqrt(prec_rows + 0.1)
    return (theta * inv_root).astype(BF16)


def dot(a, b):
    return jnp.dot(a, b, preferred_element_type=F32)


def dot_t(a, b):
    return lax.dot_general(a, b, (((0,), (0,)), ((), ())), preferred_element_type=F32)


def square(a):
    wide = a.astype(F32)
    return (wide * wide).astype(BF16)


def one_hot(idx, n_rows):
    return (idx[:, None] == jnp.arange(n_rows, dtype=jnp.int32)[None, :]).astype(BF16)


def row_sums(idx, go, n_rows):
    hot = one_hot(idx, n_rows)
    return dot_t(hot, go), dot_t(hot, square(go))


def slopes(pre, total, total_sq):
    sig = jax.nn.sigmoid(pre)
    h = sig * (1.0 + pre * (1.0 - sig))
    return (h * total).astype(BF16), (h * h * total_sq).astype(BF16)


def update(grad, sq_sum, mean, precision):
    new_precision = 0.7 * precision + 0.3 * sq_sum
    new_mean = mean - 0.5 * (grad + 0.1 * mean) / (new_precision + 0.1)
    return new_mean, new_precision


def own_sample(mean, precision, block_salts, dp_pos, shard_pos, n_shard, width):
    rows_blk, cols_blk = mean.shape
    inv_root = 1.0 / jnp.sqrt(F32(width))
    salt = lax.dynamic_index_in_dim(block_salts, dp_pos * n_shard + shard_pos, 0, keepdims=False)
    return sample_block(
        mean, precision, dp_pos * rows_blk, shard_pos * cols_blk, salt, cols_blk * n_shard, inv_root
    )


def general(table, indices, grad_out, mean, precision, block_salts):
    n_dp, n_shard = lax.axis_size("dp"), lax.axis_size("shard")
    dp_pos, shard_pos = lax.axis_index("dp"), lax.axis_index("shard")
    n_rows, width = table.shape[0], table.shape[1] * n_shard
    rows_blk = mean.shape[0]
    whole = lax.all_gather(table, "shard", axis=1, tiled=True)
    tab = lax.dynamic_slice_in_dim(whole, dp_pos * rows_blk, rows_blk, 1)
    weight = own_sample(mean, precision, block_salts, dp_pos, shard_pos, n_shard, width)
    pre = lax.psum_scatter(dot(tab, weight), "dp", scatter_dimension=1, tiled=True)
    go = lax.all_to_all(grad_out, "dp", 1, 0, tiled=True)
    idx = lax.all_gather(indices, "dp", axis=0, tiled=True)
    s, s2 = slopes(pre, *row_sums(idx, go, n_rows))
    s = lax.all_gather(s, "dp", axis=1, tiled=True)
    s2 = lax.all_gather(s2, "dp", axis=1, tiled=True)
    grad = dot_t(tab, s) * (1.0 / jnp.sqrt(F32(width)))
    sq_sum = dot_t(square(tab), s2) * (1.0 / F32(width))
    return update(grad, sq_sum, mean, precision)


CORE = [(j, j ^ 1) for j in range(4)]
CHIP = [(j, j ^ 2) for j in range(4)]
CROSS = [(j, j ^ 3) for j in range(4)]


def table_moves():
    near = [((0, 0), (1, 0)), ((0, 1), (2, 0)), ((1, 0), (0, 1)), ((1, 1), (2, 1))]
    far = [((0, 0), (3, 0)), ((1, 0), (3, 1))]
    both = []
    for moves in (near, far):
        pairs = []
        for (z, d), (z2, d2) in moves:
            pairs.append((z * 4 + d, z2 * 4 + d2))
            pairs.append(((3 - z) * 4 + 3 - d, (3 - z2) * 4 + 3 - d2))
        both.append(pairs)
    return both


TILE = 256
VMEM_LIMIT = 60 * 1024 * 1024
FINAL_LIMIT = 28 * 1024 * 1024


def call(kernel, scalars, grid, ins, outs, deps=(), scratch=(), alias=None, limit=VMEM_LIMIT, cost=(1, 1)):
    n_in, n_out, n_dep = len(ins), len(outs), len(deps)

    def body(*refs):
        sc = refs[0]
        in_refs = refs[1 : 1 + n_in]
        rest = refs[1 + n_in + n_dep :]
        kernel(sc, in_refs, rest[:n_out], rest[n_out:])

    in_specs = [pl.BlockSpec(b, m) for _, b, m in ins]
    in_specs += [pl.BlockSpec(memory_space=pl.ANY)] * n_dep
    got = pl.pallas_call(
        body,
        grid_spec=pltpu.PrefetchScalarGridSpec(
            num_scalar_prefetch=1,
            grid=grid,
            in_specs=in_specs,
            out_specs=[pl.BlockSpec(b, m) for _, _, b, m in outs],
            scratch_shapes=list(scratch),
        ),
        out_shape=[jax.ShapeDtypeStruct(s, d) for s, d, _, _ in outs],
        input_output_aliases={1 + n_in + i: o for i, o in (alias or {}).items()},
        compiler_params=pltpu.CompilerParams(vmem_limit_bytes=VMEM_LIMIT),
        cost_estimate=pl.CostEstimate(flops=cost[0], bytes_accessed=cost[1], transcendentals=0),
    )(scalars, *[a for a, _, _ in ins], *deps)
    return got


def after(x, *deps):
    return lax.optimization_barrier((x, *deps))[0]


def sample_parts(scal, mean, precision, part, full_ff, width, deps=()):
    rows, _ = mean.shape
    step, strip = rows // 2, 16
    flips = (3, 1, 2, 0)
    inv_root = 1.0 / (width ** 0.5)

    def flip_of(g):
        return jnp.where(g == 0, flips[0], jnp.where(g == 1, flips[1], jnp.where(g == 2, flips[2], flips[3])))

    def kernel(sc, ins, outs, scratch):
        g, r = pl.program_id(0), pl.program_id(1)
        start = (sc[2] + r * step) * full_ff + sc[3] + (sc[0] ^ flip_of(g)) * part
        salt = sc[1]
        base = (
            lax.broadcasted_iota(jnp.int32, (strip, part), 0) * full_ff
            + lax.broadcasted_iota(jnp.int32, (strip, part), 1)
        )

        def strip_of(n):
            at = pl.ds(pl.multiple_of(n * strip, strip), strip)
            mixed = (base + (start + n * (strip * full_ff))) ^ salt
            mixed = mixed * 73244475
            mixed = mixed ^ ((mixed & 2147483647) >> 16)
            mixed = mixed * 73244475
            mixed = mixed ^ ((mixed & 2147483647) >> 16)
            kept = ((mixed & 2147483647) >> 7).astype(F32)
            noise = 1.7320508075688772 * (2.0 * (kept + 0.5) / 16777216.0 - 1.0)
            theta = ins[0][at, :] + 0.5 * noise * lax.rsqrt(ins[1][at, :] + 0.1)
            return at, (theta * inv_root).astype(BF16)

        for m in range(4):
            @pl.when(g == m)
            def _(m=m):
                @pl.loop(0, step // strip)
                def _(n):
                    at, w = strip_of(n)
                    outs[m][at, :] = w

    last = rows // step - 1
    block = (step, part)
    source = lambda g, r, sc: (r, sc[0] ^ flip_of(g))

    def target(m):
        return lambda g, r, sc: (jnp.where(g == m, r, jnp.where(g < m, 0, last)), 0)

    return call(
        kernel, scal, (4, rows // step),
        [(mean, block, source), (precision, block, source)],
        [((rows, part), BF16, block, target(m)) for m in range(4)],
        deps,
    )


def sum_rows(scal, groups, n_rows, part, before=None, deps=()):
    ins = []
    for idx, go, flip in groups:
        count = idx.shape[0]
        ins.append((idx.reshape(1, count), (1, count), lambda i, sc: (0, 0)))
        if flip is None:
            ins.append((go, (count, part), lambda i, sc: (0, 0)))
        else:
            ins.append((go, (count, part), lambda i, sc, f=flip: (0, sc[0] ^ f)))
    n = len(groups)
    tile = (TILE, part)
    if before is not None:
        ins += [(b, tile, lambda i, sc: (i, 0)) for b in before]

    def kernel(sc, ins, outs, scratch):
        i = pl.program_id(0)

        @pl.when(i == 0)
        def _():
            for g in range(n):
                @pl.loop(0, ins[2 * g + 1].shape[0] // 64)
                def _(k):
                    at = pl.ds(pl.multiple_of(k * 64, 64), 64)
                    wide = ins[2 * g + 1][at, :].astype(F32)
                    scratch[g][at, :] = (wide * wide).astype(BF16)

        start = lax.rem(i * TILE + sc[4], n_rows)
        total = total_sq = None
        if before is not None:
            total, total_sq = ins[2 * n][...], ins[2 * n + 1][...]
        for g in range(n):
            idx = ins[2 * g][...]
            row = start + lax.broadcasted_iota(jnp.int32, (TILE, idx.shape[1]), 0)
            hot = jnp.where(row == idx, 1.0, 0.0).astype(BF16)
            a, b = dot(hot, ins[2 * g + 1][...]), dot(hot, scratch[g][...])
            total = a if total is None else total + a
            total_sq = b if total_sq is None else total_sq + b
        outs[0][...] = total
        outs[1][...] = total_sq

    return call(
        kernel, scal, (n_rows // TILE,), ins,
        [((n_rows, part), F32, tile, lambda i, sc: (i, 0))] * 2,
        deps, scratch=[pltpu.VMEM((idx.shape[0], part), BF16) for idx, _, _ in groups],
    )


def final(scal, tab_t, tab_t_sq, pieces, mean, precision, part, width, before):
    rows, half = tab_t[0].shape
    cut = pieces[0][0][0][0].shape[1]
    n = len(pieces)
    inv_root, inv_width = 1.0 / (width ** 0.5), 1.0 / width

    def kernel(sc, ins, outs, scratch):
        for m in range(n):
            @pl.when(pl.program_id(0) == m)
            def _(m=m):
                sa, qa, sb, qb = ins[6 + 4 * m : 10 + 4 * m]
                grad = dot(ins[0][...], sa[...]) + dot(ins[1][...], sb[...])
                sq_sum = dot(ins[2][...], qa[...]) + dot(ins[3][...], qb[...])
                outs[0][...], outs[1][...] = update(grad * inv_root, sq_sum * inv_width, ins[4][...], ins[5][...])

    def place(p, sc):
        at = [(sc[0] ^ flip) * part + start for _, flip, start in pieces]
        out = at[0]
        for m in range(1, n):
            out = jnp.where(p == m, at[m], out)
        return 0, pl.multiple_of(out, 128)

    whole = lambda p, sc: (0, 0)
    block = (pl.Element(rows), pl.Element(cut))
    slots = [slot for quads, _, _ in pieces for slot in quads]
    return call(
        kernel, scal, (n,),
        [(a, a.shape, whole) for a in (*tab_t, *tab_t_sq)]
        + [(mean, block, place), (precision, block, place)]
        + [(s, (half, cut), lambda p, sc, h=h: (h, 0)) for s, h in slots],
        [(mean.shape, F32, block, place)] * 2,
        tuple(before),
        alias={0: 0, 1: 1} if before else None,
        limit=FINAL_LIMIT,
    )


def on_device(table, indices, grad_out, mean, precision, block_salts):
    n_shard = lax.axis_size("shard")
    dp_pos, shard_pos = lax.axis_index("dp"), lax.axis_index("shard")
    member = lax.axis_index("members")
    n_rows, width = table.shape[0], table.shape[1] * n_shard
    rows_blk, cols_blk = mean.shape
    count = indices.shape[0]
    part = cols_blk // 4
    half, few, most = n_rows // 2, count // 2, count * 3 // 4
    salt = lax.dynamic_index_in_dim(block_salts, dp_pos * n_shard + shard_pos, 0, keepdims=False)
    scal = jnp.stack([dp_pos, salt, dp_pos * rows_blk, shard_pos * cols_blk, member * half]).astype(jnp.int32)
    both = ("shard", "dp")
    to_near, to_far = table_moves()
    sync = lax.optimization_barrier

    def cols(a, flip, row, rows):
        return lax.dynamic_slice(a, (row, (dp_pos ^ flip) * part), (rows, part))

    idx_core, idx_chip, idx_cross = (lax.ppermute(indices, "dp", p) for p in (CORE, CHIP, CROSS))
    own_a = lax.dynamic_slice_in_dim(table, member * half, half, 0)
    near_a = lax.ppermute(own_a, both, to_near)
    far_a = lax.ppermute(own_a, both, to_far)
    x1 = cols(after(grad_out, own_a), 2, 0, count)
    x1, idx_core, idx_chip, idx_cross = sync((x1, idx_core, idx_chip, idx_cross))
    x1_in = lax.ppermute(x1, "dp", CHIP)
    x2 = cols(after(grad_out, x1), 3, 0, most)
    x2_in = lax.ppermute(x2, "dp", CROSS)
    go1 = after(grad_out, x2)
    go_mine = [cols(go1, 1, r, few) for r in (0, few)]
    go_core = [lax.ppermute(g, "dp", CORE) for g in go_mine]
    w_far_send, w_near_send, w_far, w_near = sample_parts(
        scal, mean, precision, part, cols_blk * n_shard, width, go_core
    )
    groups = [(indices, grad_out, 0), (idx_core[:few], go_core[0], None), (idx_core[few:], go_core[1], None)]
    sums = sum_rows(scal, groups, n_rows, part, None, [w_near])
    x3 = cols(after(grad_out, *sums), 3, most, count - most)
    x1_in, x2_in, near_a, far_a, w_far_send, w_near_send, w_far, w_near, s0, s1, x3 = sync(
        (x1_in, x2_in, near_a, far_a, w_far_send, w_near_send, w_far, w_near, *sums, x3)
    )
    tab_a = jnp.where(shard_pos == dp_pos, own_a, near_a + far_a)
    tab_b = lax.ppermute(tab_a, "members", [(0, 1), (1, 0)])
    core_a = lax.ppermute(tab_a, "dp", CORE)
    w_core_far = lax.ppermute(w_far_send, "dp", CORE)
    w_core_near = lax.ppermute(w_near_send, "dp", CORE)
    out_a = (dot(tab_a, w_far) + dot(core_a, w_core_far)).astype(BF16)
    pre_a = lax.ppermute(out_a, "dp", CHIP)
    own_pre_a = dot(after(tab_a, out_a), w_near) + dot(core_a, w_core_near)
    x3_in = lax.ppermute(x3, "dp", CROSS)
    groups = [(idx_chip, x1_in, None), (idx_cross[:most], x2_in, None), (idx_cross[most:], x3_in, None)]
    sums = sum_rows(scal, groups, n_rows, part, (s0, s1), [own_pre_a])
    pre_a, tab_b, s0, s1 = sync((pre_a, tab_b, *sums))
    quarter = half // 2
    core_b = [lax.ppermute(t, "dp", CORE) for t in (tab_b[:quarter], tab_b[quarter:])]
    core_b = jnp.concatenate(core_b, 0)
    out_b = (dot(tab_b, w_far) + dot(core_b, w_core_far)).astype(BF16)
    pre_b = lax.ppermute(out_b, "dp", CHIP)
    pre_a, pb = after(pre_a, out_b), after(tab_b, out_b)
    own_pre_b = dot(pb, w_near) + dot(core_b, w_core_near)

    cut = part // 2
    starts = (0, cut)

    def slopes_of(f, n, h, k):
        r, c = slice(h * half, (h + 1) * half), slice(starts[k], starts[k] + cut)
        return slopes(f[:, c].astype(F32) + n[:, c], s0[r, c], s1[r, c])

    send_a = jnp.concatenate([*slopes_of(pre_a, own_pre_a, 0, 0), *slopes_of(pre_a, own_pre_a, 0, 1)], 0)
    far_a = lax.ppermute(send_a, "dp", CHIP)
    pre_b, send_a, own_pre_b = sync((pre_b, send_a, own_pre_b))
    b0 = slopes_of(pre_b, own_pre_b, 1, 0)
    last = jnp.concatenate(slopes_of(after(pre_b, *b0), own_pre_b, 1, 1), 0)

    far_b0 = [lax.ppermute(s, "dp", CHIP) for s in b0]
    far_last = lax.ppermute(last, "dp", CHIP)
    core_a2 = lax.ppermute(send_a, "dp", CORE)
    core_b0 = [lax.ppermute(s, "dp", CORE) for s in b0]
    core_last = lax.ppermute(last, "dp", CORE)
    t0, t1 = after(tab_a, last).T, after(tab_b, last).T
    tab_t, tab_t_sq = (t0, t1), (square(t0), square(t1))

    def write(outs, *pieces):
        return final(scal, tab_t, tab_t_sq, pieces, mean, precision, part, width, outs)

    def chunk0(a, b, flip):
        return [(a, 0), (a, 1), (b[0], 0), (b[1], 0)], flip, starts[0]

    def chunk1(a, b, flip):
        return [(a, 2), (a, 3), (b, 0), (b, 1)], flip, starts[1]

    outs = write(
        (), chunk0(send_a, b0, 0), chunk1(send_a, last, 0), chunk0(core_a2, core_b0, 1), chunk1(core_a2, core_last, 1)
    )
    far_a, far_b0 = after(far_a, *outs), [after(s, *outs) for s in far_b0]
    fwd_a = lax.ppermute(far_a, "dp", CORE)
    fwd_b0 = [lax.ppermute(s, "dp", CORE) for s in far_b0]
    outs = write(outs, chunk0(far_a, far_b0, 2), chunk0(fwd_a, fwd_b0, 3))
    far_last = after(far_last, *outs)
    fwd_last = lax.ppermute(far_last, "dp", CORE)
    outs = write(outs, chunk1(far_a, far_last, 2), chunk1(fwd_a, fwd_last, 3))
    return tuple(outs)


def solution(mesh):
    in_specs = (
        P(None, "shard"),
        P(("members", "dp")),
        P(("members", "dp"), "shard"),
        P(("members", "dp"), "shard"),
        P(("members", "dp"), "shard"),
        P("members"),
    )
    out_specs = (P(("members", "dp"), "shard"), P(("members", "dp"), "shard"))
    fits = mesh.shape["dp"] == 4 and mesh.shape["shard"] == 4
    return jax.shard_map(
        on_device if fits else general,
        mesh=mesh,
        in_specs=in_specs,
        out_specs=out_specs,
        check_vma=False,
    )
```

```python
import functools

import jax
import jax.numpy as jnp
from jax import lax
from jax.experimental import pallas as pl
from jax.experimental.pallas import tpu as pltpu
from jax.sharding import PartitionSpec as P

F32 = jnp.float32
BF16 = jnp.bfloat16


def hashed_noise(rows, cols, salt_value, full_ff):
    value = rows * full_ff + cols
    mixed = jnp.bitwise_xor(value, salt_value)
    mixed = mixed * 73244475
    mixed = jnp.bitwise_xor(mixed, jnp.right_shift(jnp.bitwise_and(mixed, 2147483647), 16))
    mixed = mixed * 73244475
    mixed = jnp.bitwise_xor(mixed, jnp.right_shift(jnp.bitwise_and(mixed, 2147483647), 16))
    kept = jnp.right_shift(jnp.bitwise_and(mixed, 2147483647), 7).astype(jnp.float32)
    return 1.7320508075688772 * (2.0 * (kept + 0.5) / 16777216.0 - 1.0)


def sample_block(mean_rows, prec_rows, row_start, col_start, salt_rows, full_ff, inv_root):
    rows = row_start + jnp.arange(mean_rows.shape[0], dtype=jnp.int32)[:, None]
    cols = col_start + jnp.arange(mean_rows.shape[1], dtype=jnp.int32)[None, :]
    noise = hashed_noise(rows, cols, salt_rows, full_ff)
    theta = mean_rows + 0.5 * noise / jnp.sqrt(prec_rows + 0.1)
    return (theta * inv_root).astype(BF16)


def dot(a, b):
    return jnp.dot(a, b, preferred_element_type=F32)


def dot_t(a, b):
    return lax.dot_general(a, b, (((0,), (0,)), ((), ())), preferred_element_type=F32)


def square(a):
    wide = a.astype(F32)
    return (wide * wide).astype(BF16)


def one_hot(idx, n_rows):
    return (idx[:, None] == jnp.arange(n_rows, dtype=jnp.int32)[None, :]).astype(BF16)


def row_sums(idx, go, n_rows):
    hot = one_hot(idx, n_rows)
    return dot_t(hot, go), dot_t(hot, square(go))


def slopes(pre, total, total_sq):
    sig = jax.nn.sigmoid(pre)
    h = sig * (1.0 + pre * (1.0 - sig))
    return (h * total).astype(BF16), (h * h * total_sq).astype(BF16)


def update(grad, sq_sum, mean, precision):
    new_precision = 0.7 * precision + 0.3 * sq_sum
    new_mean = mean - 0.5 * (grad + 0.1 * mean) / (new_precision + 0.1)
    return new_mean, new_precision


def own_sample(mean, precision, block_salts, dp_pos, shard_pos, n_shard, width):
    rows_blk, cols_blk = mean.shape
    inv_root = 1.0 / jnp.sqrt(F32(width))
    salt = lax.dynamic_index_in_dim(block_salts, dp_pos * n_shard + shard_pos, 0, keepdims=False)
    return sample_block(
        mean, precision, dp_pos * rows_blk, shard_pos * cols_blk, salt, cols_blk * n_shard, inv_root
    )


def general(table, indices, grad_out, mean, precision, block_salts):
    n_dp, n_shard = lax.axis_size("dp"), lax.axis_size("shard")
    dp_pos, shard_pos = lax.axis_index("dp"), lax.axis_index("shard")
    n_rows, width = table.shape[0], table.shape[1] * n_shard
    rows_blk = mean.shape[0]
    whole = lax.all_gather(table, "shard", axis=1, tiled=True)
    tab = lax.dynamic_slice_in_dim(whole, dp_pos * rows_blk, rows_blk, 1)
    weight = own_sample(mean, precision, block_salts, dp_pos, shard_pos, n_shard, width)
    pre = lax.psum_scatter(dot(tab, weight), "dp", scatter_dimension=1, tiled=True)
    go = lax.all_to_all(grad_out, "dp", 1, 0, tiled=True)
    idx = lax.all_gather(indices, "dp", axis=0, tiled=True)
    s, s2 = slopes(pre, *row_sums(idx, go, n_rows))
    s = lax.all_gather(s, "dp", axis=1, tiled=True)
    s2 = lax.all_gather(s2, "dp", axis=1, tiled=True)
    grad = dot_t(tab, s) * (1.0 / jnp.sqrt(F32(width)))
    sq_sum = dot_t(square(tab), s2) * (1.0 / F32(width))
    return update(grad, sq_sum, mean, precision)


CORE = [(j, j ^ 1) for j in range(4)]
CHIP = [(j, j ^ 2) for j in range(4)]
CROSS = [(j, j ^ 3) for j in range(4)]


def table_moves():
    near = [((0, 0), (1, 0)), ((0, 1), (2, 0)), ((1, 0), (0, 1)), ((1, 1), (2, 1))]
    far = [((0, 0), (3, 0)), ((1, 0), (3, 1))]
    both = []
    for moves in (near, far):
        pairs = []
        for (z, d), (z2, d2) in moves:
            pairs.append((z * 4 + d, z2 * 4 + d2))
            pairs.append(((3 - z) * 4 + 3 - d, (3 - z2) * 4 + 3 - d2))
        both.append(pairs)
    return both


TILE = 256
VMEM_LIMIT = 60 * 1024 * 1024
FINAL_LIMIT = 28 * 1024 * 1024


def call(kernel, scalars, grid, ins, outs, deps=(), scratch=(), alias=None, limit=VMEM_LIMIT, cost=(1, 1)):
    n_in, n_out, n_dep = len(ins), len(outs), len(deps)

    def body(*refs):
        sc = refs[0]
        in_refs = refs[1 : 1 + n_in]
        rest = refs[1 + n_in + n_dep :]
        kernel(sc, in_refs, rest[:n_out], rest[n_out:])

    in_specs = [pl.BlockSpec(b, m) for _, b, m in ins]
    in_specs += [pl.BlockSpec(memory_space=pl.ANY)] * n_dep
    got = pl.pallas_call(
        body,
        grid_spec=pltpu.PrefetchScalarGridSpec(
            num_scalar_prefetch=1,
            grid=grid,
            in_specs=in_specs,
            out_specs=[pl.BlockSpec(b, m) for _, _, b, m in outs],
            scratch_shapes=list(scratch),
        ),
        out_shape=[jax.ShapeDtypeStruct(s, d) for s, d, _, _ in outs],
        input_output_aliases={1 + n_in + i: o for i, o in (alias or {}).items()},
        compiler_params=pltpu.CompilerParams(vmem_limit_bytes=VMEM_LIMIT),
        cost_estimate=pl.CostEstimate(flops=cost[0], bytes_accessed=cost[1], transcendentals=0),
    )(scalars, *[a for a, _, _ in ins], *deps)
    return got


def after(x, *deps):
    return lax.optimization_barrier((x, *deps))[0]


def sample_parts(scal, mean, precision, part, full_ff, width, deps=()):
    rows, _ = mean.shape
    step, strip = rows // 2, 16
    flips = (3, 1, 2, 0)
    inv_root = 1.0 / (width ** 0.5)

    def flip_of(g):
        return jnp.where(g == 0, flips[0], jnp.where(g == 1, flips[1], jnp.where(g == 2, flips[2], flips[3])))

    def kernel(sc, ins, outs, scratch):
        g, r = pl.program_id(0), pl.program_id(1)
        start = (sc[2] + r * step) * full_ff + sc[3] + (sc[0] ^ flip_of(g)) * part
        salt = sc[1]
        base = (
            lax.broadcasted_iota(jnp.int32, (strip, part), 0) * full_ff
            + lax.broadcasted_iota(jnp.int32, (strip, part), 1)
        )

        def strip_of(n):
            at = pl.ds(pl.multiple_of(n * strip, strip), strip)
            mixed = (base + (start + n * (strip * full_ff))) ^ salt
            mixed = mixed * 73244475
            mixed = mixed ^ ((mixed & 2147483647) >> 16)
            mixed = mixed * 73244475
            mixed = mixed ^ ((mixed & 2147483647) >> 16)
            kept = ((mixed & 2147483647) >> 7).astype(F32)
            noise = 1.7320508075688772 * (2.0 * (kept + 0.5) / 16777216.0 - 1.0)
            theta = ins[0][at, :] + 0.5 * noise * lax.rsqrt(ins[1][at, :] + 0.1)
            return at, (theta * inv_root).astype(BF16)

        for m in range(4):
            @pl.when(g == m)
            def _(m=m):
                @pl.loop(0, step // strip)
                def _(n):
                    at, w = strip_of(n)
                    outs[m][at, :] = w

    last = rows // step - 1
    block = (step, part)
    source = lambda g, r, sc: (r, sc[0] ^ flip_of(g))

    def target(m):
        return lambda g, r, sc: (jnp.where(g == m, r, jnp.where(g < m, 0, last)), 0)

    return call(
        kernel, scal, (4, rows // step),
        [(mean, block, source), (precision, block, source)],
        [((rows, part), BF16, block, target(m)) for m in range(4)],
        deps,
    )


def sum_rows(scal, groups, n_rows, part, before=None, deps=()):
    ins = []
    for idx, go, flip in groups:
        count = idx.shape[0]
        ins.append((idx.reshape(1, count), (1, count), lambda i, sc: (0, 0)))
        if flip is None:
            ins.append((go, (count, part), lambda i, sc: (0, 0)))
        else:
            ins.append((go, (count, part), lambda i, sc, f=flip: (0, sc[0] ^ f)))
    n = len(groups)
    tile = (TILE, part)
    if before is not None:
        ins += [(b, tile, lambda i, sc: (i, 0)) for b in before]

    def kernel(sc, ins, outs, scratch):
        i = pl.program_id(0)

        @pl.when(i == 0)
        def _():
            for g in range(n):
                @pl.loop(0, ins[2 * g + 1].shape[0] // 64)
                def _(k):
                    at = pl.ds(pl.multiple_of(k * 64, 64), 64)
                    wide = ins[2 * g + 1][at, :].astype(F32)
                    scratch[g][at, :] = (wide * wide).astype(BF16)

        start = lax.rem(i * TILE + sc[4], n_rows)
        total = total_sq = None
        if before is not None:
            total, total_sq = ins[2 * n][...], ins[2 * n + 1][...]
        for g in range(n):
            idx = ins[2 * g][...]
            row = start + lax.broadcasted_iota(jnp.int32, (TILE, idx.shape[1]), 0)
            hot = jnp.where(row == idx, 1.0, 0.0).astype(BF16)
            a, b = dot(hot, ins[2 * g + 1][...]), dot(hot, scratch[g][...])
            total = a if total is None else total + a
            total_sq = b if total_sq is None else total_sq + b
        outs[0][...] = total
        outs[1][...] = total_sq

    return call(
        kernel, scal, (n_rows // TILE,), ins,
        [((n_rows, part), F32, tile, lambda i, sc: (i, 0))] * 2,
        deps, scratch=[pltpu.VMEM((idx.shape[0], part), BF16) for idx, _, _ in groups],
    )


def final(scal, tab_t, tab_t_sq, pieces, mean, precision, part, width, before):
    rows, half = tab_t[0].shape
    cut = pieces[0][0][0][0].shape[1]
    n = len(pieces)
    inv_root, inv_width = 1.0 / (width ** 0.5), 1.0 / width

    def kernel(sc, ins, outs, scratch):
        for m in range(n):
            @pl.when(pl.program_id(0) == m)
            def _(m=m):
                sa, qa, sb, qb = ins[6 + 4 * m : 10 + 4 * m]
                grad = dot(ins[0][...], sa[...]) + dot(ins[1][...], sb[...])
                sq_sum = dot(ins[2][...], qa[...]) + dot(ins[3][...], qb[...])
                outs[0][...], outs[1][...] = update(grad * inv_root, sq_sum * inv_width, ins[4][...], ins[5][...])

    def place(p, sc):
        at = [(sc[0] ^ flip) * part + start for _, flip, start in pieces]
        out = at[0]
        for m in range(1, n):
            out = jnp.where(p == m, at[m], out)
        return 0, pl.multiple_of(out, 128)

    whole = lambda p, sc: (0, 0)
    block = (pl.Element(rows), pl.Element(cut))
    slots = [slot for quads, _, _ in pieces for slot in quads]
    return call(
        kernel, scal, (n,),
        [(a, a.shape, whole) for a in (*tab_t, *tab_t_sq)]
        + [(mean, block, place), (precision, block, place)]
        + [(s, (half, cut), lambda p, sc, h=h: (h, 0)) for s, h in slots],
        [(mean.shape, F32, block, place)] * 2,
        tuple(before),
        alias={0: 0, 1: 1} if before else None,
        limit=FINAL_LIMIT,
    )


def on_device(table, indices, grad_out, mean, precision, block_salts):
    n_shard = lax.axis_size("shard")
    dp_pos, shard_pos = lax.axis_index("dp"), lax.axis_index("shard")
    member = lax.axis_index("members")
    n_rows, width = table.shape[0], table.shape[1] * n_shard
    rows_blk, cols_blk = mean.shape
    count = indices.shape[0]
    part = cols_blk // 4
    half, few = n_rows // 2, count // 2
    salt = lax.dynamic_index_in_dim(block_salts, dp_pos * n_shard + shard_pos, 0, keepdims=False)
    scal = jnp.stack([dp_pos, salt, dp_pos * rows_blk, shard_pos * cols_blk, member * half]).astype(jnp.int32)
    both = ("shard", "dp")
    to_near, to_far = table_moves()
    sync = lax.optimization_barrier

    def cols(a, flip, row, rows):
        return lax.dynamic_slice(a, (row, (dp_pos ^ flip) * part), (rows, part))

    idx_core, idx_chip, idx_cross = (lax.ppermute(indices, "dp", p) for p in (CORE, CHIP, CROSS))
    own_a = lax.dynamic_slice_in_dim(table, member * half, half, 0)
    near_a = lax.ppermute(own_a, both, to_near)
    far_a = lax.ppermute(own_a, both, to_far)
    x1 = cols(after(grad_out, own_a), 2, 0, count)
    x1, idx_core, idx_chip, idx_cross = sync((x1, idx_core, idx_chip, idx_cross))
    x1_in = lax.ppermute(x1, "dp", CHIP)
    x2 = cols(after(grad_out, x1), 3, 0, count)
    x2_in = lax.ppermute(x2, "dp", CROSS)
    go1 = after(grad_out, x2)
    go_mine = [cols(go1, 1, r, few) for r in (0, few)]
    go_core = [lax.ppermute(g, "dp", CORE) for g in go_mine]
    w_far_send, w_near_send, w_far, w_near = sample_parts(
        scal, mean, precision, part, cols_blk * n_shard, width, go_core
    )
    groups = [(indices, grad_out, 0), (idx_core[:few], go_core[0], None), (idx_core[few:], go_core[1], None)]
    sums = sum_rows(scal, groups, n_rows, part, None, [w_near])
    x1_in, near_a, far_a, w_far_send, w_near_send, w_far, w_near, s0, s1 = sync(
        (x1_in, near_a, far_a, w_far_send, w_near_send, w_far, w_near, *sums)
    )
    tab_a = jnp.where(shard_pos == dp_pos, own_a, near_a + far_a)
    tab_b = lax.ppermute(tab_a, "members", [(0, 1), (1, 0)])
    core_a = lax.ppermute(tab_a, "dp", CORE)
    w_core_far = lax.ppermute(w_far_send, "dp", CORE)
    w_core_near = lax.ppermute(w_near_send, "dp", CORE)
    core_a, w_core_far, x2_in = sync((core_a, w_core_far, x2_in))
    out_a = (dot(tab_a, w_far) + dot(core_a, w_core_far)).astype(BF16)
    pre_a = lax.ppermute(out_a, "dp", CHIP)
    sums = sum_rows(scal, [(idx_chip, x1_in, None), (idx_cross, x2_in, None)], n_rows, part, (s0, s1), [out_a])
    tab_b, s0, s1 = sync((tab_b, *sums))
    quarter = half // 2
    core_b = [lax.ppermute(t, "dp", CORE) for t in (tab_b[:quarter], tab_b[quarter:])]
    core_b, pre_a = sync((core_b, pre_a))
    core_b = jnp.concatenate(core_b, 0)
    out_b = (dot(tab_b, w_far) + dot(core_b, w_core_far)).astype(BF16)
    pre_b = lax.ppermute(out_b, "dp", CHIP)
    pre_a, pb = after(pre_a, out_b), after(tab_b, out_b)
    own_pre_a = dot(after(tab_a, out_b), w_near) + dot(core_a, w_core_near)
    own_pre_b = dot(pb, w_near) + dot(core_b, w_core_near)

    cut = part // 2
    starts = (0, cut)

    def slopes_of(f, n, h, k):
        r, c = slice(h * half, (h + 1) * half), slice(starts[k], starts[k] + cut)
        return slopes(f[:, c].astype(F32) + n[:, c], s0[r, c], s1[r, c])

    send_a = jnp.concatenate([*slopes_of(pre_a, own_pre_a, 0, 0), *slopes_of(pre_a, own_pre_a, 0, 1)], 0)
    far_a = lax.ppermute(send_a, "dp", CHIP)
    pre_b, send_a, own_pre_b = sync((pre_b, send_a, own_pre_b))
    b0 = slopes_of(pre_b, own_pre_b, 1, 0)
    last = jnp.concatenate(slopes_of(after(pre_b, *b0), own_pre_b, 1, 1), 0)

    far_b0 = [lax.ppermute(s, "dp", CHIP) for s in b0]
    far_last = lax.ppermute(last, "dp", CHIP)
    core_a2 = lax.ppermute(send_a, "dp", CORE)
    core_b0 = [lax.ppermute(s, "dp", CORE) for s in b0]
    core_last = lax.ppermute(last, "dp", CORE)
    t0, t1 = after(tab_a, last).T, after(tab_b, last).T
    tab_t, tab_t_sq = (t0, t1), (square(t0), square(t1))

    def write(outs, *pieces):
        return final(scal, tab_t, tab_t_sq, pieces, mean, precision, part, width, outs)

    def chunk0(a, b, flip):
        return [(a, 0), (a, 1), (b[0], 0), (b[1], 0)], flip, starts[0]

    def chunk1(a, b, flip):
        return [(a, 2), (a, 3), (b, 0), (b, 1)], flip, starts[1]

    outs = write(
        (), chunk0(send_a, b0, 0), chunk1(send_a, last, 0), chunk0(core_a2, core_b0, 1), chunk1(core_a2, core_last, 1)
    )
    far_a, far_b0 = after(far_a, *outs), [after(s, *outs) for s in far_b0]
    fwd_a = lax.ppermute(far_a, "dp", CORE)
    fwd_b0 = [lax.ppermute(s, "dp", CORE) for s in far_b0]
    outs = write(outs, chunk0(far_a, far_b0, 2), chunk0(fwd_a, fwd_b0, 3))
    far_last = after(far_last, *outs)
    fwd_last = lax.ppermute(far_last, "dp", CORE)
    outs = write(outs, chunk1(far_a, far_last, 2), chunk1(fwd_a, fwd_last, 3))
    return tuple(outs)


def solution(mesh):
    in_specs = (
        P(None, "shard"),
        P(("members", "dp")),
        P(("members", "dp"), "shard"),
        P(("members", "dp"), "shard"),
        P(("members", "dp"), "shard"),
        P("members"),
    )
    out_specs = (P(("members", "dp"), "shard"), P(("members", "dp"), "shard"))
    fits = mesh.shape["dp"] == 4 and mesh.shape["shard"] == 4
    return jax.shard_map(
        on_device if fits else general,
        mesh=mesh,
        in_specs=in_specs,
        out_specs=out_specs,
        check_vma=False,
    )
```

```python
import functools

import jax
import jax.numpy as jnp
from jax import lax
from jax.experimental import pallas as pl
from jax.experimental.pallas import tpu as pltpu
from jax.sharding import PartitionSpec as P

F32 = jnp.float32
BF16 = jnp.bfloat16


def hashed_noise(rows, cols, salt_value, full_ff):
    value = rows * full_ff + cols
    mixed = jnp.bitwise_xor(value, salt_value)
    mixed = mixed * 73244475
    mixed = jnp.bitwise_xor(mixed, jnp.right_shift(jnp.bitwise_and(mixed, 2147483647), 16))
    mixed = mixed * 73244475
    mixed = jnp.bitwise_xor(mixed, jnp.right_shift(jnp.bitwise_and(mixed, 2147483647), 16))
    kept = jnp.right_shift(jnp.bitwise_and(mixed, 2147483647), 7).astype(jnp.float32)
    return 1.7320508075688772 * (2.0 * (kept + 0.5) / 16777216.0 - 1.0)


def sample_block(mean_rows, prec_rows, row_start, col_start, salt_rows, full_ff, inv_root):
    rows = row_start + jnp.arange(mean_rows.shape[0], dtype=jnp.int32)[:, None]
    cols = col_start + jnp.arange(mean_rows.shape[1], dtype=jnp.int32)[None, :]
    noise = hashed_noise(rows, cols, salt_rows, full_ff)
    theta = mean_rows + 0.5 * noise / jnp.sqrt(prec_rows + 0.1)
    return (theta * inv_root).astype(BF16)


def dot(a, b):
    return jnp.dot(a, b, preferred_element_type=F32)


def dot_t(a, b):
    return lax.dot_general(a, b, (((0,), (0,)), ((), ())), preferred_element_type=F32)


def square(a):
    wide = a.astype(F32)
    return (wide * wide).astype(BF16)


def one_hot(idx, n_rows):
    return (idx[:, None] == jnp.arange(n_rows, dtype=jnp.int32)[None, :]).astype(BF16)


def row_sums(idx, go, n_rows):
    hot = one_hot(idx, n_rows)
    return dot_t(hot, go), dot_t(hot, square(go))


def slopes(pre, total, total_sq):
    sig = jax.nn.sigmoid(pre)
    h = sig * (1.0 + pre * (1.0 - sig))
    return (h * total).astype(BF16), (h * h * total_sq).astype(BF16)


def update(grad, sq_sum, mean, precision):
    new_precision = 0.7 * precision + 0.3 * sq_sum
    new_mean = mean - 0.5 * (grad + 0.1 * mean) / (new_precision + 0.1)
    return new_mean, new_precision


def own_sample(mean, precision, block_salts, dp_pos, shard_pos, n_shard, width):
    rows_blk, cols_blk = mean.shape
    inv_root = 1.0 / jnp.sqrt(F32(width))
    salt = lax.dynamic_index_in_dim(block_salts, dp_pos * n_shard + shard_pos, 0, keepdims=False)
    return sample_block(
        mean, precision, dp_pos * rows_blk, shard_pos * cols_blk, salt, cols_blk * n_shard, inv_root
    )


def general(table, indices, grad_out, mean, precision, block_salts):
    n_dp, n_shard = lax.axis_size("dp"), lax.axis_size("shard")
    dp_pos, shard_pos = lax.axis_index("dp"), lax.axis_index("shard")
    n_rows, width = table.shape[0], table.shape[1] * n_shard
    rows_blk = mean.shape[0]
    whole = lax.all_gather(table, "shard", axis=1, tiled=True)
    tab = lax.dynamic_slice_in_dim(whole, dp_pos * rows_blk, rows_blk, 1)
    weight = own_sample(mean, precision, block_salts, dp_pos, shard_pos, n_shard, width)
    pre = lax.psum_scatter(dot(tab, weight), "dp", scatter_dimension=1, tiled=True)
    go = lax.all_to_all(grad_out, "dp", 1, 0, tiled=True)
    idx = lax.all_gather(indices, "dp", axis=0, tiled=True)
    s, s2 = slopes(pre, *row_sums(idx, go, n_rows))
    s = lax.all_gather(s, "dp", axis=1, tiled=True)
    s2 = lax.all_gather(s2, "dp", axis=1, tiled=True)
    grad = dot_t(tab, s) * (1.0 / jnp.sqrt(F32(width)))
    sq_sum = dot_t(square(tab), s2) * (1.0 / F32(width))
    return update(grad, sq_sum, mean, precision)


CORE = [(j, j ^ 1) for j in range(4)]
CHIP = [(j, j ^ 2) for j in range(4)]
CROSS = [(j, j ^ 3) for j in range(4)]


def table_moves():
    near = [((0, 0), (1, 0)), ((0, 1), (2, 0)), ((1, 0), (0, 1)), ((1, 1), (2, 1))]
    far = [((0, 0), (3, 0)), ((1, 0), (3, 1))]
    both = []
    for moves in (near, far):
        pairs = []
        for (z, d), (z2, d2) in moves:
            pairs.append((z * 4 + d, z2 * 4 + d2))
            pairs.append(((3 - z) * 4 + 3 - d, (3 - z2) * 4 + 3 - d2))
        both.append(pairs)
    return both


TILE = 256
VMEM_LIMIT = 60 * 1024 * 1024
FINAL_LIMIT = 28 * 1024 * 1024


def call(kernel, scalars, grid, ins, outs, deps=(), scratch=(), alias=None, alias_in=None, limit=VMEM_LIMIT, cost=(1, 1)):
    n_in, n_out, n_dep = len(ins), len(outs), len(deps)

    def body(*refs):
        sc = refs[0]
        in_refs = refs[1 : 1 + n_in]
        rest = refs[1 + n_in + n_dep :]
        kernel(sc, in_refs, rest[:n_out], rest[n_out:])

    in_specs = [pl.BlockSpec(b, m) for _, b, m in ins]
    in_specs += [pl.BlockSpec(memory_space=pl.ANY)] * n_dep
    got = pl.pallas_call(
        body,
        grid_spec=pltpu.PrefetchScalarGridSpec(
            num_scalar_prefetch=1,
            grid=grid,
            in_specs=in_specs,
            out_specs=[pl.BlockSpec(b, m) for _, _, b, m in outs],
            scratch_shapes=list(scratch),
        ),
        out_shape=[jax.ShapeDtypeStruct(s, d) for s, d, _, _ in outs],
        input_output_aliases={1 + n_in + i: o for i, o in (alias or {}).items()}
        | {1 + i: o for i, o in (alias_in or {}).items()},
        compiler_params=pltpu.CompilerParams(vmem_limit_bytes=VMEM_LIMIT),
        cost_estimate=pl.CostEstimate(flops=cost[0], bytes_accessed=cost[1], transcendentals=0),
    )(scalars, *[a for a, _, _ in ins], *deps)
    return got


def after(x, *deps):
    return lax.optimization_barrier((x, *deps))[0]


def sample_parts(scal, mean, precision, part, full_ff, width, deps=()):
    rows, _ = mean.shape
    step, strip = rows // 2, 16
    flips = (3, 1, 2, 0)
    inv_root = 1.0 / (width ** 0.5)

    def flip_of(g):
        return jnp.where(g == 0, flips[0], jnp.where(g == 1, flips[1], jnp.where(g == 2, flips[2], flips[3])))

    def kernel(sc, ins, outs, scratch):
        g, r = pl.program_id(0), pl.program_id(1)
        start = (sc[2] + r * step) * full_ff + sc[3] + (sc[0] ^ flip_of(g)) * part
        salt = sc[1]
        base = (
            lax.broadcasted_iota(jnp.int32, (strip, part), 0) * full_ff
            + lax.broadcasted_iota(jnp.int32, (strip, part), 1)
        )

        def strip_of(n):
            at = pl.ds(pl.multiple_of(n * strip, strip), strip)
            mixed = (base + (start + n * (strip * full_ff))) ^ salt
            mixed = mixed * 73244475
            mixed = mixed ^ ((mixed & 2147483647) >> 16)
            mixed = mixed * 73244475
            mixed = mixed ^ ((mixed & 2147483647) >> 16)
            kept = ((mixed & 2147483647) >> 7).astype(F32)
            noise = 1.7320508075688772 * (2.0 * (kept + 0.5) / 16777216.0 - 1.0)
            theta = ins[0][at, :] + 0.5 * noise * lax.rsqrt(ins[1][at, :] + 0.1)
            return at, (theta * inv_root).astype(BF16)

        for m in range(4):
            @pl.when(g == m)
            def _(m=m):
                @pl.loop(0, step // strip)
                def _(n):
                    at, w = strip_of(n)
                    outs[m][at, :] = w

    last = rows // step - 1
    block = (step, part)
    source = lambda g, r, sc: (r, sc[0] ^ flip_of(g))

    def target(m):
        return lambda g, r, sc: (jnp.where(g == m, r, jnp.where(g < m, 0, last)), 0)

    return call(
        kernel, scal, (4, rows // step),
        [(mean, block, source), (precision, block, source)],
        [((rows, part), BF16, block, target(m)) for m in range(4)],
        deps,
    )


def sum_rows(scal, groups, n_rows, part, before=None, deps=()):
    ins = []
    for idx, go, flip in groups:
        count = idx.shape[0]
        ins.append((idx.reshape(1, count), (1, count), lambda i, sc: (0, 0)))
        if flip is None:
            ins.append((go, (count, part), lambda i, sc: (0, 0)))
        else:
            ins.append((go, (count, part), lambda i, sc, f=flip: (0, sc[0] ^ f)))
    n = len(groups)
    tile = (TILE, part)
    if before is not None:
        ins += [(b, tile, lambda i, sc: (i, 0)) for b in before]

    def kernel(sc, ins, outs, scratch):
        i = pl.program_id(0)

        @pl.when(i == 0)
        def _():
            for g in range(n):
                @pl.loop(0, ins[2 * g + 1].shape[0] // 64)
                def _(k):
                    at = pl.ds(pl.multiple_of(k * 64, 64), 64)
                    wide = ins[2 * g + 1][at, :].astype(F32)
                    scratch[g][at, :] = (wide * wide).astype(BF16)

        start = lax.rem(i * TILE + sc[4], n_rows)
        total = total_sq = None
        if before is not None:
            total, total_sq = ins[2 * n][...], ins[2 * n + 1][...]
        for g in range(n):
            idx = ins[2 * g][...]
            row = start + lax.broadcasted_iota(jnp.int32, (TILE, idx.shape[1]), 0)
            hot = jnp.where(row == idx, 1.0, 0.0).astype(BF16)
            a, b = dot(hot, ins[2 * g + 1][...]), dot(hot, scratch[g][...])
            total = a if total is None else total + a
            total_sq = b if total_sq is None else total_sq + b
        outs[0][...] = total
        outs[1][...] = total_sq

    return call(
        kernel, scal, (n_rows // TILE,), ins,
        [((n_rows, part), F32, tile, lambda i, sc: (i, 0))] * 2,
        deps, scratch=[pltpu.VMEM((idx.shape[0], part), BF16) for idx, _, _ in groups],
    )


def final(scal, tab_t, tab_t_sq, pieces, mean, precision, part, width, before):
    rows, half = tab_t[0].shape
    cut = pieces[0][0][0][0].shape[1]
    n = len(pieces)
    inv_root, inv_width = 1.0 / (width ** 0.5), 1.0 / width

    def kernel(sc, ins, outs, scratch):
        for m in range(n):
            @pl.when(pl.program_id(0) == m)
            def _(m=m):
                sa, qa, sb, qb = ins[6 + 4 * m : 10 + 4 * m]
                grad = dot(ins[0][...], sa[...]) + dot(ins[1][...], sb[...])
                sq_sum = dot(ins[2][...], qa[...]) + dot(ins[3][...], qb[...])
                outs[0][...], outs[1][...] = update(grad * inv_root, sq_sum * inv_width, ins[4][...], ins[5][...])

    def place(p, sc):
        at = [(sc[0] ^ flip) * part + start for _, flip, start in pieces]
        out = at[0]
        for m in range(1, n):
            out = jnp.where(p == m, at[m], out)
        return 0, pl.multiple_of(out, 128)

    whole = lambda p, sc: (0, 0)
    block = (pl.Element(rows), pl.Element(cut))
    slots = [slot for quads, _, _ in pieces for slot in quads]
    return call(
        kernel, scal, (n,),
        [(a, a.shape, whole) for a in (*tab_t, *tab_t_sq)]
        + [(mean, block, place), (precision, block, place)]
        + [(s, (half, cut), lambda p, sc, h=h: (h, 0)) for s, h in slots],
        [(mean.shape, F32, block, place)] * 2,
        tuple(before),
        alias={0: 0, 1: 1} if before else None,
        limit=FINAL_LIMIT,
    )


def final_halves(scal, tab_t, tab_t_sq, pieces, mean, precision, part, width, before, second):
    rows, half = tab_t.shape
    cut = pieces[0][0][0][0].shape[1]
    n = len(pieces)
    inv_root, inv_width = 1.0 / (width ** 0.5), 1.0 / width
    state = (mean, *before) if second else (precision,)
    first_s = 2 + len(state)

    def kernel(sc, ins, outs, scratch):
        for m in range(n):
            @pl.when(pl.program_id(0) == m)
            def _(m=m):
                grad = dot(ins[0][...], ins[first_s + 2 * m][...]) * inv_root
                sq_sum = dot(ins[1][...], ins[first_s + 1 + 2 * m][...]) * (0.3 * inv_width)
                if second:
                    old = ins[2][...]
                    new_precision = ins[4][...] + sq_sum
                    outs[0][...] = old - 0.5 * (ins[3][...] + grad + 0.1 * old) / (new_precision + 0.1)
                    outs[1][...] = new_precision
                else:
                    outs[0][...] = grad
                    outs[1][...] = 0.7 * ins[2][...] + sq_sum

    def place(p, sc):
        at = [(sc[0] ^ flip) * part + start for _, flip, start in pieces]
        out = at[0]
        for m in range(1, n):
            out = jnp.where(p == m, at[m], out)
        return 0, pl.multiple_of(out, 128)

    whole = lambda p, sc: (0, 0)
    block = (pl.Element(rows), pl.Element(cut))
    slots = [slot for pair, _, _ in pieces for slot in pair]
    return call(
        kernel, scal, (n,),
        [(a, a.shape, whole) for a in (tab_t, tab_t_sq)]
        + [(a, block, place) for a in state]
        + [(s, (half, cut), lambda p, sc, h=h: (h, 0)) for s, h in slots],
        [(mean.shape, F32, block, place)] * 2,
        () if second else tuple(before),
        alias=None if second else {0: 0, 1: 1},
        alias_in={3: 0, 4: 1} if second else None,
        limit=FINAL_LIMIT,
    )


def on_device(table, indices, grad_out, mean, precision, block_salts):
    n_shard = lax.axis_size("shard")
    dp_pos, shard_pos = lax.axis_index("dp"), lax.axis_index("shard")
    member = lax.axis_index("members")
    n_rows, width = table.shape[0], table.shape[1] * n_shard
    rows_blk, cols_blk = mean.shape
    count = indices.shape[0]
    part = cols_blk // 4
    half, few = n_rows // 2, count // 2
    salt = lax.dynamic_index_in_dim(block_salts, dp_pos * n_shard + shard_pos, 0, keepdims=False)
    scal = jnp.stack([dp_pos, salt, dp_pos * rows_blk, shard_pos * cols_blk, member * half]).astype(jnp.int32)
    both = ("shard", "dp")
    to_near, to_far = table_moves()
    sync = lax.optimization_barrier

    def cols(a, flip, row, rows):
        return lax.dynamic_slice(a, (row, (dp_pos ^ flip) * part), (rows, part))

    idx_core, idx_chip, idx_cross = (lax.ppermute(indices, "dp", p) for p in (CORE, CHIP, CROSS))
    own_a = lax.dynamic_slice_in_dim(table, member * half, half, 0)
    near_a = lax.ppermute(own_a, both, to_near)
    far_a = lax.ppermute(own_a, both, to_far)
    x1 = cols(after(grad_out, own_a), 2, 0, count)
    x1, idx_core, idx_chip, idx_cross = sync((x1, idx_core, idx_chip, idx_cross))
    x1_in = lax.ppermute(x1, "dp", CHIP)
    x2 = cols(after(grad_out, x1), 3, 0, count)
    x2_in = lax.ppermute(x2, "dp", CROSS)
    go1 = after(grad_out, x2)
    go_mine = [cols(go1, 1, r, few) for r in (0, few)]
    go_core = [lax.ppermute(g, "dp", CORE) for g in go_mine]
    w_far_send, w_near_send, w_far, w_near = sample_parts(
        scal, mean, precision, part, cols_blk * n_shard, width, go_core
    )
    groups = [(indices, grad_out, 0), (idx_core[:few], go_core[0], None), (idx_core[few:], go_core[1], None)]
    sums = sum_rows(scal, groups, n_rows, part, None, [w_near])
    x1_in, near_a, far_a, w_far_send, w_near_send, w_far, w_near, s0, s1 = sync(
        (x1_in, near_a, far_a, w_far_send, w_near_send, w_far, w_near, *sums)
    )
    tab_a = jnp.where(shard_pos == dp_pos, own_a, near_a + far_a)
    tab_b = lax.ppermute(tab_a, "members", [(0, 1), (1, 0)])
    core_a = lax.ppermute(tab_a, "dp", CORE)
    w_core_far = lax.ppermute(w_far_send, "dp", CORE)
    w_core_near = lax.ppermute(w_near_send, "dp", CORE)
    core_a, w_core_far, x2_in = sync((core_a, w_core_far, x2_in))
    out_a = (dot(tab_a, w_far) + dot(core_a, w_core_far)).astype(BF16)
    pre_a = lax.ppermute(out_a, "dp", CHIP)
    sums = sum_rows(scal, [(idx_chip, x1_in, None), (idx_cross, x2_in, None)], n_rows, part, (s0, s1), [out_a])
    tab_b, s0, s1 = sync((tab_b, *sums))
    quarter = half // 2
    core_b = [lax.ppermute(t, "dp", CORE) for t in (tab_b[:quarter], tab_b[quarter:])]
    core_b, pre_a = sync((core_b, pre_a))
    core_b = jnp.concatenate(core_b, 0)
    out_b = (dot(tab_b, w_far) + dot(core_b, w_core_far)).astype(BF16)
    pre_b = lax.ppermute(out_b, "dp", CHIP)
    pre_a, pb = after(pre_a, out_b), after(tab_b, out_b)
    own_pre_a = dot(after(tab_a, out_b), w_near) + dot(core_a, w_core_near)
    own_pre_b = dot(pb, w_near) + dot(core_b, w_core_near)

    cut = part // 2
    starts = (0, cut)

    def slopes_of(f, n, h, k):
        r, c = slice(h * half, (h + 1) * half), slice(starts[k], starts[k] + cut)
        return slopes(f[:, c].astype(F32) + n[:, c], s0[r, c], s1[r, c])

    send_a = jnp.concatenate([*slopes_of(pre_a, own_pre_a, 0, 0), *slopes_of(pre_a, own_pre_a, 0, 1)], 0)
    far_a = lax.ppermute(send_a, "dp", CHIP)
    pre_b, send_a, own_pre_b = sync((pre_b, send_a, own_pre_b))
    b0 = slopes_of(pre_b, own_pre_b, 1, 0)
    last = jnp.concatenate(slopes_of(after(pre_b, *b0), own_pre_b, 1, 1), 0)

    far_b0 = [lax.ppermute(s, "dp", CHIP) for s in b0]
    far_last = lax.ppermute(last, "dp", CHIP)
    core_a2 = lax.ppermute(send_a, "dp", CORE)
    core_b0 = [lax.ppermute(s, "dp", CORE) for s in b0]
    core_last = lax.ppermute(last, "dp", CORE)
    t0, t1 = after(tab_a, last).T, after(tab_b, last).T
    tab_t, tab_t_sq = (t0, t1), (square(t0), square(t1))

    def write(outs, *pieces):
        return final(scal, tab_t, tab_t_sq, pieces, mean, precision, part, width, outs)

    def chunk0(a, b, flip):
        return [(a, 0), (a, 1), (b[0], 0), (b[1], 0)], flip, starts[0]

    def chunk1(a, b, flip):
        return [(a, 2), (a, 3), (b, 0), (b, 1)], flip, starts[1]

    outs = write(
        (), chunk0(send_a, b0, 0), chunk1(send_a, last, 0), chunk0(core_a2, core_b0, 1), chunk1(core_a2, core_last, 1)
    )
    far_a = after(far_a, *outs)
    fwd_a = lax.ppermute(far_a, "dp", CORE)

    def write_half(outs, second, *pieces):
        h = int(second)
        return final_halves(scal, tab_t[h], tab_t_sq[h], pieces, mean, precision, part, width, outs, second)

    pairs = [[(s, 2 * k), (s, 2 * k + 1)] for s in (far_a, fwd_a) for k in (0, 1)]
    outs = write_half(
        outs, False, (pairs[0], 2, starts[0]), (pairs[1], 2, starts[1]), (pairs[2], 3, starts[0]), (pairs[3], 3, starts[1])
    )
    far_b0 = [after(s, *outs) for s in far_b0]
    fwd_b0 = [lax.ppermute(s, "dp", CORE) for s in far_b0]
    outs = write_half(
        outs, True, ([(s, 0) for s in far_b0], 2, starts[0]), ([(s, 0) for s in fwd_b0], 3, starts[0])
    )
    far_last = after(far_last, *outs)
    fwd_last = lax.ppermute(far_last, "dp", CORE)
    outs = write_half(
        outs, True, ([(far_last, 0), (far_last, 1)], 2, starts[1]), ([(fwd_last, 0), (fwd_last, 1)], 3, starts[1])
    )
    return tuple(outs)


def solution(mesh):
    in_specs = (
        P(None, "shard"),
        P(("members", "dp")),
        P(("members", "dp"), "shard"),
        P(("members", "dp"), "shard"),
        P(("members", "dp"), "shard"),
        P("members"),
    )
    out_specs = (P(("members", "dp"), "shard"), P(("members", "dp"), "shard"))
    fits = mesh.shape["dp"] == 4 and mesh.shape["shard"] == 4
    return jax.shard_map(
        on_device if fits else general,
        mesh=mesh,
        in_specs=in_specs,
        out_specs=out_specs,
        check_vma=False,
    )
```

```python
import functools

import jax
import jax.numpy as jnp
from jax import lax
from jax.experimental import pallas as pl
from jax.experimental.pallas import tpu as pltpu
from jax.sharding import PartitionSpec as P

F32 = jnp.float32
BF16 = jnp.bfloat16


def hashed_noise(rows, cols, salt_value, full_ff):
    value = rows * full_ff + cols
    mixed = jnp.bitwise_xor(value, salt_value)
    mixed = mixed * 73244475
    mixed = jnp.bitwise_xor(mixed, jnp.right_shift(jnp.bitwise_and(mixed, 2147483647), 16))
    mixed = mixed * 73244475
    mixed = jnp.bitwise_xor(mixed, jnp.right_shift(jnp.bitwise_and(mixed, 2147483647), 16))
    kept = jnp.right_shift(jnp.bitwise_and(mixed, 2147483647), 7).astype(jnp.float32)
    return 1.7320508075688772 * (2.0 * (kept + 0.5) / 16777216.0 - 1.0)


def sample_block(mean_rows, prec_rows, row_start, col_start, salt_rows, full_ff, inv_root):
    rows = row_start + jnp.arange(mean_rows.shape[0], dtype=jnp.int32)[:, None]
    cols = col_start + jnp.arange(mean_rows.shape[1], dtype=jnp.int32)[None, :]
    noise = hashed_noise(rows, cols, salt_rows, full_ff)
    theta = mean_rows + 0.5 * noise / jnp.sqrt(prec_rows + 0.1)
    return (theta * inv_root).astype(BF16)


def dot(a, b):
    return jnp.dot(a, b, preferred_element_type=F32)


def dot_t(a, b):
    return lax.dot_general(a, b, (((0,), (0,)), ((), ())), preferred_element_type=F32)


def square(a):
    wide = a.astype(F32)
    return (wide * wide).astype(BF16)


def one_hot(idx, n_rows):
    return (idx[:, None] == jnp.arange(n_rows, dtype=jnp.int32)[None, :]).astype(BF16)


def row_sums(idx, go, n_rows):
    hot = one_hot(idx, n_rows)
    return dot_t(hot, go), dot_t(hot, square(go))


def slopes(pre, total, total_sq):
    sig = jax.nn.sigmoid(pre)
    h = sig * (1.0 + pre * (1.0 - sig))
    return (h * total).astype(BF16), (h * h * total_sq).astype(BF16)


def update(grad, sq_sum, mean, precision):
    new_precision = 0.7 * precision + 0.3 * sq_sum
    new_mean = mean - 0.5 * (grad + 0.1 * mean) / (new_precision + 0.1)
    return new_mean, new_precision


def own_sample(mean, precision, block_salts, dp_pos, shard_pos, n_shard, width):
    rows_blk, cols_blk = mean.shape
    inv_root = 1.0 / jnp.sqrt(F32(width))
    salt = lax.dynamic_index_in_dim(block_salts, dp_pos * n_shard + shard_pos, 0, keepdims=False)
    return sample_block(
        mean, precision, dp_pos * rows_blk, shard_pos * cols_blk, salt, cols_blk * n_shard, inv_root
    )


def general(table, indices, grad_out, mean, precision, block_salts):
    n_dp, n_shard = lax.axis_size("dp"), lax.axis_size("shard")
    dp_pos, shard_pos = lax.axis_index("dp"), lax.axis_index("shard")
    n_rows, width = table.shape[0], table.shape[1] * n_shard
    rows_blk = mean.shape[0]
    whole = lax.all_gather(table, "shard", axis=1, tiled=True)
    tab = lax.dynamic_slice_in_dim(whole, dp_pos * rows_blk, rows_blk, 1)
    weight = own_sample(mean, precision, block_salts, dp_pos, shard_pos, n_shard, width)
    pre = lax.psum_scatter(dot(tab, weight), "dp", scatter_dimension=1, tiled=True)
    go = lax.all_to_all(grad_out, "dp", 1, 0, tiled=True)
    idx = lax.all_gather(indices, "dp", axis=0, tiled=True)
    s, s2 = slopes(pre, *row_sums(idx, go, n_rows))
    s = lax.all_gather(s, "dp", axis=1, tiled=True)
    s2 = lax.all_gather(s2, "dp", axis=1, tiled=True)
    grad = dot_t(tab, s) * (1.0 / jnp.sqrt(F32(width)))
    sq_sum = dot_t(square(tab), s2) * (1.0 / F32(width))
    return update(grad, sq_sum, mean, precision)


CORE = [(j, j ^ 1) for j in range(4)]
CHIP = [(j, j ^ 2) for j in range(4)]
CROSS = [(j, j ^ 3) for j in range(4)]


def table_moves():
    near = [((0, 0), (1, 0)), ((0, 1), (2, 0)), ((1, 0), (0, 1)), ((1, 1), (2, 1))]
    far = [((0, 0), (3, 0)), ((1, 0), (3, 1))]
    both = []
    for moves in (near, far):
        pairs = []
        for (z, d), (z2, d2) in moves:
            pairs.append((z * 4 + d, z2 * 4 + d2))
            pairs.append(((3 - z) * 4 + 3 - d, (3 - z2) * 4 + 3 - d2))
        both.append(pairs)
    return both


TILE = 256
VMEM_LIMIT = 60 * 1024 * 1024
FINAL_LIMIT = 28 * 1024 * 1024


def call(kernel, scalars, grid, ins, outs, deps=(), scratch=(), alias=None, alias_in=None, limit=VMEM_LIMIT, cost=(1, 1)):
    n_in, n_out, n_dep = len(ins), len(outs), len(deps)

    def body(*refs):
        sc = refs[0]
        in_refs = refs[1 : 1 + n_in]
        rest = refs[1 + n_in + n_dep :]
        kernel(sc, in_refs, rest[:n_out], rest[n_out:])

    in_specs = [pl.BlockSpec(b, m) for _, b, m in ins]
    in_specs += [pl.BlockSpec(memory_space=pl.ANY)] * n_dep
    got = pl.pallas_call(
        body,
        grid_spec=pltpu.PrefetchScalarGridSpec(
            num_scalar_prefetch=1,
            grid=grid,
            in_specs=in_specs,
            out_specs=[pl.BlockSpec(b, m) for _, _, b, m in outs],
            scratch_shapes=list(scratch),
        ),
        out_shape=[jax.ShapeDtypeStruct(s, d) for s, d, _, _ in outs],
        input_output_aliases={1 + n_in + i: o for i, o in (alias or {}).items()}
        | {1 + i: o for i, o in (alias_in or {}).items()},
        compiler_params=pltpu.CompilerParams(vmem_limit_bytes=VMEM_LIMIT),
        cost_estimate=pl.CostEstimate(flops=cost[0], bytes_accessed=cost[1], transcendentals=0),
    )(scalars, *[a for a, _, _ in ins], *deps)
    return got


def after(x, *deps):
    return lax.optimization_barrier((x, *deps))[0]


def sample_parts(scal, mean, precision, part, full_ff, width, deps=()):
    rows, _ = mean.shape
    step, strip = rows // 2, 16
    flips = (3, 1, 2, 0)
    inv_root = 1.0 / (width ** 0.5)

    def flip_of(g):
        return jnp.where(g == 0, flips[0], jnp.where(g == 1, flips[1], jnp.where(g == 2, flips[2], flips[3])))

    def kernel(sc, ins, outs, scratch):
        g, r = pl.program_id(0), pl.program_id(1)
        start = (sc[2] + r * step) * full_ff + sc[3] + (sc[0] ^ flip_of(g)) * part
        salt = sc[1]
        base = (
            lax.broadcasted_iota(jnp.int32, (strip, part), 0) * full_ff
            + lax.broadcasted_iota(jnp.int32, (strip, part), 1)
        )

        def strip_of(n):
            at = pl.ds(pl.multiple_of(n * strip, strip), strip)
            mixed = (base + (start + n * (strip * full_ff))) ^ salt
            mixed = mixed * 73244475
            mixed = mixed ^ ((mixed & 2147483647) >> 16)
            mixed = mixed * 73244475
            mixed = mixed ^ ((mixed & 2147483647) >> 16)
            kept = ((mixed & 2147483647) >> 7).astype(F32)
            noise = 1.7320508075688772 * (2.0 * (kept + 0.5) / 16777216.0 - 1.0)
            theta = ins[0][at, :] + 0.5 * noise * lax.rsqrt(ins[1][at, :] + 0.1)
            return at, (theta * inv_root).astype(BF16)

        for m in range(4):
            @pl.when(g == m)
            def _(m=m):
                @pl.loop(0, step // strip)
                def _(n):
                    at, w = strip_of(n)
                    outs[m][at, :] = w

    last = rows // step - 1
    block = (step, part)
    source = lambda g, r, sc: (r, sc[0] ^ flip_of(g))

    def target(m):
        return lambda g, r, sc: (jnp.where(g == m, r, jnp.where(g < m, 0, last)), 0)

    return call(
        kernel, scal, (4, rows // step),
        [(mean, block, source), (precision, block, source)],
        [((rows, part), BF16, block, target(m)) for m in range(4)],
        deps,
    )


def sum_rows(scal, groups, n_rows, part, before=None, deps=()):
    ins = []
    for idx, go, flip in groups:
        count = idx.shape[0]
        ins.append((idx.reshape(1, count), (1, count), lambda i, sc: (0, 0)))
        if flip is None:
            ins.append((go, (count, part), lambda i, sc: (0, 0)))
        else:
            ins.append((go, (count, part), lambda i, sc, f=flip: (0, sc[0] ^ f)))
    n = len(groups)
    tile = (TILE, part)
    if before is not None:
        ins += [(b, tile, lambda i, sc: (i, 0)) for b in before]

    def kernel(sc, ins, outs, scratch):
        i = pl.program_id(0)

        @pl.when(i == 0)
        def _():
            for g in range(n):
                @pl.loop(0, ins[2 * g + 1].shape[0] // 64)
                def _(k):
                    at = pl.ds(pl.multiple_of(k * 64, 64), 64)
                    wide = ins[2 * g + 1][at, :].astype(F32)
                    scratch[g][at, :] = (wide * wide).astype(BF16)

        start = lax.rem(i * TILE + sc[4], n_rows)
        total = total_sq = None
        if before is not None:
            total, total_sq = ins[2 * n][...], ins[2 * n + 1][...]
        for g in range(n):
            idx = ins[2 * g][...]
            row = start + lax.broadcasted_iota(jnp.int32, (TILE, idx.shape[1]), 0)
            hot = jnp.where(row == idx, 1.0, 0.0).astype(BF16)
            a, b = dot(hot, ins[2 * g + 1][...]), dot(hot, scratch[g][...])
            total = a if total is None else total + a
            total_sq = b if total_sq is None else total_sq + b
        outs[0][...] = total
        outs[1][...] = total_sq

    return call(
        kernel, scal, (n_rows // TILE,), ins,
        [((n_rows, part), F32, tile, lambda i, sc: (i, 0))] * 2,
        deps, scratch=[pltpu.VMEM((idx.shape[0], part), BF16) for idx, _, _ in groups],
    )


def final(scal, tab_t, tab_t_sq, pieces, mean, precision, part, width, before):
    rows, half = tab_t[0].shape
    cut = pieces[0][0][0][0].shape[1]
    n = len(pieces)
    inv_root, inv_width = 1.0 / (width ** 0.5), 1.0 / width

    def kernel(sc, ins, outs, scratch):
        for m in range(n):
            @pl.when(pl.program_id(0) == m)
            def _(m=m):
                sa, qa, sb, qb = ins[6 + 4 * m : 10 + 4 * m]
                grad = dot(ins[0][...], sa[...]) + dot(ins[1][...], sb[...])
                sq_sum = dot(ins[2][...], qa[...]) + dot(ins[3][...], qb[...])
                outs[0][...], outs[1][...] = update(grad * inv_root, sq_sum * inv_width, ins[4][...], ins[5][...])

    def place(p, sc):
        at = [(sc[0] ^ flip) * part + start for _, flip, start in pieces]
        out = at[0]
        for m in range(1, n):
            out = jnp.where(p == m, at[m], out)
        return 0, pl.multiple_of(out, 128)

    whole = lambda p, sc: (0, 0)
    block = (pl.Element(rows), pl.Element(cut))
    slots = [slot for quads, _, _ in pieces for slot in quads]
    return call(
        kernel, scal, (n,),
        [(a, a.shape, whole) for a in (*tab_t, *tab_t_sq)]
        + [(mean, block, place), (precision, block, place)]
        + [(s, (half, cut), lambda p, sc, h=h: (h, 0)) for s, h in slots],
        [(mean.shape, F32, block, place)] * 2,
        tuple(before),
        alias={0: 0, 1: 1} if before else None,
        limit=FINAL_LIMIT,
    )


def final_halves(scal, tab_t, tab_t_sq, pieces, mean, precision, part, width, before, second):
    rows, half = tab_t.shape
    cut = pieces[0][0][0][0].shape[1]
    n = len(pieces)
    inv_root, inv_width = 1.0 / (width ** 0.5), 1.0 / width
    state = (mean, *before) if second else (precision,)
    first_s = 2 + len(state)

    def kernel(sc, ins, outs, scratch):
        for m in range(n):
            @pl.when(pl.program_id(0) == m)
            def _(m=m):
                grad = dot(ins[0][...], ins[first_s + 2 * m][...]) * inv_root
                sq_sum = dot(ins[1][...], ins[first_s + 1 + 2 * m][...]) * (0.3 * inv_width)
                if second:
                    old = ins[2][...]
                    new_precision = ins[4][...] + sq_sum
                    outs[0][...] = old - 0.5 * (ins[3][...] + grad + 0.1 * old) / (new_precision + 0.1)
                    outs[1][...] = new_precision
                else:
                    outs[0][...] = grad
                    outs[1][...] = 0.7 * ins[2][...] + sq_sum

    def place(p, sc):
        at = [(sc[0] ^ flip) * part + start for _, flip, start in pieces]
        out = at[0]
        for m in range(1, n):
            out = jnp.where(p == m, at[m], out)
        return 0, pl.multiple_of(out, 128)

    whole = lambda p, sc: (0, 0)
    block = (pl.Element(rows), pl.Element(cut))
    slots = [slot for pair, _, _ in pieces for slot in pair]
    return call(
        kernel, scal, (n,),
        [(a, a.shape, whole) for a in (tab_t, tab_t_sq)]
        + [(a, block, place) for a in state]
        + [(s, (half, cut), lambda p, sc, h=h: (h, 0)) for s, h in slots],
        [(mean.shape, F32, block, place)] * 2,
        () if second else tuple(before),
        alias=None if second else {0: 0, 1: 1},
        alias_in={3: 0, 4: 1} if second else None,
        limit=FINAL_LIMIT,
    )


def on_device(table, indices, grad_out, mean, precision, block_salts):
    n_shard = lax.axis_size("shard")
    dp_pos, shard_pos = lax.axis_index("dp"), lax.axis_index("shard")
    member = lax.axis_index("members")
    n_rows, width = table.shape[0], table.shape[1] * n_shard
    rows_blk, cols_blk = mean.shape
    count = indices.shape[0]
    part = cols_blk // 4
    half, few = n_rows // 2, count // 2
    salt = lax.dynamic_index_in_dim(block_salts, dp_pos * n_shard + shard_pos, 0, keepdims=False)
    scal = jnp.stack([dp_pos, salt, dp_pos * rows_blk, shard_pos * cols_blk, member * half]).astype(jnp.int32)
    both = ("shard", "dp")
    to_near, to_far = table_moves()
    sync = lax.optimization_barrier

    def cols(a, flip, row, rows):
        return lax.dynamic_slice(a, (row, (dp_pos ^ flip) * part), (rows, part))

    idx_core, idx_chip, idx_cross = (lax.ppermute(indices, "dp", p) for p in (CORE, CHIP, CROSS))
    own_a = lax.dynamic_slice_in_dim(table, member * half, half, 0)
    near_a = lax.ppermute(own_a, both, to_near)
    far_a = lax.ppermute(own_a, both, to_far)
    x1 = cols(after(grad_out, own_a), 2, 0, count)
    x1, idx_core, idx_chip, idx_cross = sync((x1, idx_core, idx_chip, idx_cross))
    x1_in = lax.ppermute(x1, "dp", CHIP)
    x2 = cols(after(grad_out, x1), 3, 0, count)
    x2_in = lax.ppermute(x2, "dp", CROSS)
    go1 = after(grad_out, x2)
    go_mine = [cols(go1, 1, r, few) for r in (0, few)]
    go_core = [lax.ppermute(g, "dp", CORE) for g in go_mine]
    w_far_send, w_near_send, w_far, w_near = sample_parts(
        scal, mean, precision, part, cols_blk * n_shard, width, go_core
    )
    groups = [(indices, grad_out, 0), (idx_core[:few], go_core[0], None), (idx_core[few:], go_core[1], None)]
    sums = sum_rows(scal, groups, n_rows, part, None, [w_near])
    x1_in, near_a, far_a, w_far_send, w_near_send, w_far, w_near, s0, s1 = sync(
        (x1_in, near_a, far_a, w_far_send, w_near_send, w_far, w_near, *sums)
    )
    tab_a = jnp.where(shard_pos == dp_pos, own_a, near_a + far_a)
    tab_b = lax.ppermute(tab_a, "members", [(0, 1), (1, 0)])
    core_a = lax.ppermute(tab_a, "dp", CORE)
    w_core_far = lax.ppermute(w_far_send, "dp", CORE)
    w_core_near = lax.ppermute(w_near_send, "dp", CORE)
    out_a = dot(tab_a, w_far)
    core_a, w_core_far, x2_in, out_a = sync((core_a, w_core_far, x2_in, out_a))
    out_a = (out_a + dot(core_a, w_core_far)).astype(BF16)
    pre_a = lax.ppermute(out_a, "dp", CHIP)
    sums = sum_rows(scal, [(idx_chip, x1_in, None), (idx_cross, x2_in, None)], n_rows, part, (s0, s1), [out_a])
    tab_b, s0, s1 = sync((tab_b, *sums))
    quarter = half // 2
    core_b = [lax.ppermute(t, "dp", CORE) for t in (tab_b[:quarter], tab_b[quarter:])]
    core_b, pre_a = sync((core_b, pre_a))
    core_b = jnp.concatenate(core_b, 0)
    out_b = (dot(tab_b, w_far) + dot(core_b, w_core_far)).astype(BF16)
    pre_b = lax.ppermute(out_b, "dp", CHIP)
    pre_a, pb = after(pre_a, out_b), after(tab_b, out_b)
    own_pre_a = dot(after(tab_a, out_b), w_near) + dot(core_a, w_core_near)
    own_pre_b = dot(pb, w_near) + dot(core_b, w_core_near)

    cut = part // 2
    starts = (0, cut)

    def slopes_of(f, n, h, k):
        r, c = slice(h * half, (h + 1) * half), slice(starts[k], starts[k] + cut)
        return slopes(f[:, c].astype(F32) + n[:, c], s0[r, c], s1[r, c])

    send_a = jnp.concatenate([*slopes_of(pre_a, own_pre_a, 0, 0), *slopes_of(pre_a, own_pre_a, 0, 1)], 0)
    far_a = lax.ppermute(send_a, "dp", CHIP)
    pre_b, send_a, own_pre_b = sync((pre_b, send_a, own_pre_b))
    b0 = slopes_of(pre_b, own_pre_b, 1, 0)
    last = jnp.concatenate(slopes_of(after(pre_b, *b0), own_pre_b, 1, 1), 0)

    far_b0 = [lax.ppermute(s, "dp", CHIP) for s in b0]
    far_last = lax.ppermute(last, "dp", CHIP)
    core_a2 = lax.ppermute(send_a, "dp", CORE)
    core_b0 = [lax.ppermute(s, "dp", CORE) for s in b0]
    core_last = lax.ppermute(last, "dp", CORE)
    t0, t1 = after(tab_a, last).T, after(tab_b, last).T
    tab_t, tab_t_sq = (t0, t1), (square(t0), square(t1))

    def write(outs, *pieces):
        return final(scal, tab_t, tab_t_sq, pieces, mean, precision, part, width, outs)

    def chunk0(a, b, flip):
        return [(a, 0), (a, 1), (b[0], 0), (b[1], 0)], flip, starts[0]

    def chunk1(a, b, flip):
        return [(a, 2), (a, 3), (b, 0), (b, 1)], flip, starts[1]

    outs = write(
        (), chunk0(send_a, b0, 0), chunk1(send_a, last, 0), chunk0(core_a2, core_b0, 1), chunk1(core_a2, core_last, 1)
    )
    far_a = after(far_a, *outs)
    fwd_a = lax.ppermute(far_a, "dp", CORE)

    def write_half(outs, second, *pieces):
        h = int(second)
        return final_halves(scal, tab_t[h], tab_t_sq[h], pieces, mean, precision, part, width, outs, second)

    pairs = [[(s, 2 * k), (s, 2 * k + 1)] for s in (far_a, fwd_a) for k in (0, 1)]
    outs = write_half(
        outs, False, (pairs[0], 2, starts[0]), (pairs[1], 2, starts[1]), (pairs[2], 3, starts[0]), (pairs[3], 3, starts[1])
    )
    far_b0 = [after(s, *outs) for s in far_b0]
    fwd_b0 = [lax.ppermute(s, "dp", CORE) for s in far_b0]
    outs = write_half(
        outs, True, ([(s, 0) for s in far_b0], 2, starts[0]), ([(s, 0) for s in fwd_b0], 3, starts[0])
    )
    far_last = after(far_last, *outs)
    fwd_last = lax.ppermute(far_last, "dp", CORE)
    outs = write_half(
        outs, True, ([(far_last, 0), (far_last, 1)], 2, starts[1]), ([(fwd_last, 0), (fwd_last, 1)], 3, starts[1])
    )
    return tuple(outs)


def solution(mesh):
    in_specs = (
        P(None, "shard"),
        P(("members", "dp")),
        P(("members", "dp"), "shard"),
        P(("members", "dp"), "shard"),
        P(("members", "dp"), "shard"),
        P("members"),
    )
    out_specs = (P(("members", "dp"), "shard"), P(("members", "dp"), "shard"))
    fits = mesh.shape["dp"] == 4 and mesh.shape["shard"] == 4
    return jax.shard_map(
        on_device if fits else general,
        mesh=mesh,
        in_specs=in_specs,
        out_specs=out_specs,
        check_vma=False,
    )
```
